128 devices in a mesh: tok: 4 (over z), lat: 32 (over y, x, core).
Axes of the slice: x: 4, y: 4, z: 4, core: 2. Of those that a mesh axis runs over, the one named last changes fastest.
Arguments:
- residuals: bfloat16 [2048, 4096], P('tok', 'lat'), may hold values from -6 to 6
- dictionary: bfloat16 [65536, 4096], P('lat'), may hold values from -0.09375 to 0.09375
- enc_bias: float32 [65536], P('lat'), may hold values from -3 to 3
- dec_bias: float32 [4096], replicated, may hold values from -3 to 3
- tile_ids: int32 [16, 32, 4], P('tok', 'lat'), may hold values from 0 to 31, as said below
- tile_counts: int32 [16, 32], P('tok', 'lat'), may hold values from 0 to 4, as said below
Outputs:
- tile_codes: bfloat16 [16, 32, 4, 8192], P('tok', None, None, 'lat')
- reconstruction: bfloat16 [2048, 4096], P('tok', 'lat')
- decoder_grad: float32 [65536, 4096], P('lat', 'tok')
The draws below stay inside these ranges and needn't reach their ends.
Inputs may be any that keep to these rules, and one draw needn't show every extreme that they name: `tile_ids`: for each token block and latent shard the 4 entries are distinct latent blocks; only the first tile_counts entries count. `tile_counts`: every draw has token blocks with all 4 slots active on every latent shard.
All inputs are finite; a program needn't handle non-finite values.
Results may differ from the reference program's by a relative error of at most 0.02.
Values may be sent and summed in bfloat16 or wider, within the bound.
No kernel may reach another device: no remote copies, remote signals or barrier semaphores. Data moves between devices by JAX's collectives and lax.ppermute only.
A program may use at most 128 MiB of HBM per device.

```python
import jax
import jax.numpy as jnp
from jax import lax

D = 4096
LAT_DEV = 2048
TOK_DEV = 512
TILE_ROWS = 128
LAT_TILE = 64
CAP = 4
LATENTS = 65536
TOKENS = 2048
TBLOCKS = 16
LBLOCKS = 32
N_TOK = 4
N_LAT = 32


def draw_tile_ids(key, part):
    key = jax.random.fold_in(key, 11)
    scores = jax.random.randint(key, (TBLOCKS, N_LAT, LBLOCKS), 0, 4096) * LBLOCKS
    scores = scores + jnp.arange(LBLOCKS, dtype=jnp.int32)[None, None, :]
    order = jnp.argsort(scores, axis=-1, stable=True)
    return order[:, :, :CAP].astype(jnp.int32)


def draw_tile_counts(key, part):
    key = jax.random.fold_in(key, 23)
    counts = jax.random.randint(key, (TBLOCKS, N_LAT), 0, CAP + 1)
    block_index = jnp.arange(TBLOCKS, dtype=jnp.int32)[:, None]
    counts = jnp.where(block_index % 5 == 0, CAP, counts)
    return counts.astype(jnp.int32)


def shard_levels(own_key, extent, split, smallest, top_value):
    factor_of, own = 1.0, jax.random.fold_in(own_key, 6)
    for axis_at, parts in split:
        steps = jnp.exp(jax.random.uniform(jax.random.fold_in(own, axis_at), (parts,), jnp.float32, smallest / len(split), top_value / len(split)))
        factor_of = factor_of * jnp.repeat(steps, extent[axis_at] // parts).reshape([-1 if axis == axis_at else 1 for axis in range(len(extent))])
    return factor_of


def centred(stream_key, dims, spread, reach, pieces=(), held_as=jnp.bfloat16):
    gain = shard_levels(stream_key, dims, pieces, -0.22, 0.18) if pieces else 1.0
    entries = jax.random.normal(stream_key, dims, jnp.float32) * spread * gain
    return jnp.minimum(jnp.maximum(entries, -reach), reach).astype(held_as)


def setup_inputs(seed: int = 0) -> dict:
    splits = jax.random.split(jax.random.key(seed), 7)
    residuals = centred(splits[0], (TOKENS, D), 1.0, 6.0, ((0, 4), (1, 32)))
    dictionary = centred(splits[1], (LATENTS, D), D ** -0.5, 0.09375, ((0, 32),))
    enc_bias = centred(splits[2], (LATENTS,), 0.5, 3.0, ((0, 32),), jnp.float32)
    dec_bias = centred(splits[3], (D,), 0.5, 3.0, (), jnp.float32)
    tile_ids = draw_tile_ids(jax.random.fold_in(splits[6], 71), 0)
    tile_counts = draw_tile_counts(jax.random.fold_in(splits[6], 71), 0)
    return {"residuals": residuals, "dictionary": dictionary, "enc_bias": enc_bias, "dec_bias": dec_bias, "tile_ids": tile_ids, "tile_counts": tile_counts}


def reference(residuals, dictionary, enc_bias, dec_bias, tile_ids, tile_counts):
    centered = (residuals.astype(jnp.float32) - dec_bias).astype(jnp.bfloat16)
    live_slots = jnp.arange(CAP, dtype=jnp.int32)[None, None, :] < tile_counts[:, :, None]
    selector = (tile_ids[:, :, :, None] == jnp.arange(LBLOCKS, dtype=jnp.int32)[None, None, None, :]) & live_slots[:, :, :, None]
    tile_active = jnp.any(selector, axis=2).astype(jnp.float32)
    selector_f = selector.astype(jnp.float32)

    def shard_step(running, shard_index):
        weights = lax.dynamic_slice_in_dim(dictionary, shard_index * LAT_DEV, LAT_DEV, 0)
        biases = lax.dynamic_slice_in_dim(enc_bias, shard_index * LAT_DEV, LAT_DEV, 0)
        preact = jnp.dot(centered, weights.T, preferred_element_type=jnp.float32) + biases
        mask_rows = jnp.take(tile_active, shard_index, axis=1)
        code_four = jnp.maximum(preact, 0.0).reshape(TBLOCKS, TILE_ROWS, LBLOCKS, LAT_TILE) * mask_rows[:, None, :, None]
        code_values = code_four.reshape(TOKENS, LAT_DEV).astype(jnp.bfloat16)
        pick_rows = jnp.take(selector_f, shard_index, axis=1)
        picked = jnp.einsum("bcl,brlk->bcrk", pick_rows, code_values.astype(jnp.float32).reshape(TBLOCKS, TILE_ROWS, LBLOCKS, LAT_TILE))
        tile_part = picked.reshape(TBLOCKS, CAP, TILE_ROWS * LAT_TILE).astype(jnp.bfloat16)
        running = running + jnp.dot(code_values, weights, preferred_element_type=jnp.float32)
        return running, (code_values, tile_part)

    start_sum = jnp.zeros((TOKENS, D), jnp.float32)
    total, (all_codes, all_tiles) = lax.scan(shard_step, start_sum, jnp.arange(N_LAT, dtype=jnp.int32))
    recon_full = total + dec_bias
    reconstruction = recon_full.astype(jnp.bfloat16)
    error = (recon_full - residuals.astype(jnp.float32)).astype(jnp.bfloat16)
    error_groups = error.reshape(N_TOK, TOK_DEV, D)

    def grad_step(carry, code_values):
        code_groups = code_values.reshape(N_TOK, TOK_DEV, LAT_DEV)
        summed = jnp.zeros((LAT_DEV, D), jnp.float32)
        for group in range(N_TOK):
            part = jnp.dot(code_groups[group].T, error_groups[group], preferred_element_type=jnp.float32)
            summed = summed + part.astype(jnp.bfloat16).astype(jnp.float32)
        return carry, summed

    unused, grads = lax.scan(grad_step, jnp.zeros((), jnp.float32), all_codes)
    decoder_grad = grads.reshape(LATENTS, D)
    tile_codes = jnp.transpose(all_tiles, (1, 0, 2, 3))
    return tile_codes, reconstruction, decoder_grad
```

```python
import jax
import jax.numpy as jnp
from jax import lax
from jax.experimental import pallas as pl
from jax.experimental.pallas import tpu as pltpu
from jax.sharding import PartitionSpec as P

TILE_ROWS = 128
LAT_TILE = 64
CAP = 4
SIDE = 4
ROWS = 512
WIDTH = 4096
PIECE = 128
SHIFTS = (0, 1, 3, 2)
BF = jnp.bfloat16
F32 = jnp.float32


def lat_of(y, x, c):
    return (y % SIDE) * 8 + (x % SIDE) * 2 + c


def chips():
    return [(y, x, c) for y in range(SIDE) for x in range(SIDE) for c in range(2)]


def short_leg(d):
    return [
        (lat_of(y, x, c), lat_of(y + d, x, c) if c == 0 else lat_of(y, x + d, c))
        for y, x, c in chips()
    ]


def long_leg(d):
    return [
        (lat_of(y, x, c), lat_of(y, x + d, c) if c == 0 else lat_of(y + d, x, c))
        for y, x, c in chips()
    ]


CORE = [(lat_of(y, x, c), lat_of(y, x, 1 - c)) for y, x, c in chips()]
TO_PLANE = [
    (z * 32 + lat_of(y, x, c), ((z + y) % SIDE) * 32 + lat_of(y, x, c))
    for z in range(SIDE)
    for y, x, c in chips()
]
TO_HOME = [
    (z * 32 + lat_of(y, x, c), z * 32 + lat_of(y + z, x, c))
    for z in range(SIDE)
    for y, x, c in chips()
]


def send(value, pairs):
    return lax.ppermute(value, "lat", pairs)


def params(mib):
    return pltpu.CompilerParams(vmem_limit_bytes=mib << 20)


def stack_kernel(a, b, c, d, out):
    for k, ref in enumerate((a, b, c, d)):
        out[k] = ref[...]


def stack4(parts):
    shape = parts[0].shape
    return pl.pallas_call(
        stack_kernel,
        out_shape=jax.ShapeDtypeStruct((4,) + shape, BF),
        compiler_params=params(8),
        name="stack4",
    )(*parts)


def gather_plane(piece):
    line = stack4([piece] + [send(piece, short_leg(d)) for d in SHIFTS[1:]])
    mine = [line] + [send(line, long_leg(d)) for d in SHIFTS[1:]]
    other = [send(v, CORE) for v in mine]
    return mine + other


def encode_kernel(
    ids, counts, where, *refs
):
    pieces = refs[:8]
    tiles = refs[8:12]
    enc_bias, dec_bias = refs[12:14]
    codes_t, tile_send, mine, other, resid, centered = refs[14:]
    b = pl.program_id(0)
    for k in range(8):
        for e in range(4):
            slot = k * 4 + e
            off = pl.multiple_of(where[slot] * PIECE, PIECE)
            raw = pieces[k][e]
            centered[:, pl.ds(off, PIECE)] = (
                raw.astype(F32) - dec_bias[:, pl.ds(off, PIECE)]
            ).astype(BF)
            if k == 0 or (k < 4 and e == 0):

                @pl.when(where[32] == slot)
                def _():
                    resid[...] = raw

    step = 512
    preact = jnp.zeros((TILE_ROWS, CAP * LAT_TILE), F32)
    for k in range(0, WIDTH, step):
        block = jnp.concatenate([t[:, k : k + step] for t in tiles], axis=0)
        preact += lax.dot_general(
            centered[:, k : k + step],
            block,
            (((1,), (1,)), ((), ())),
            preferred_element_type=F32,
        )
    bias = jnp.concatenate(
        [enc_bias[pl.ds(ids[b, s], 1), :] for s in range(CAP)], axis=1
    )
    slot_of = lax.broadcasted_iota(jnp.int32, (TILE_ROWS, CAP * LAT_TILE), 1) // LAT_TILE
    live = slot_of < counts[b]
    values = jnp.where(live, jnp.maximum(preact + bias, 0.0), 0.0)
    codes = values.astype(BF)
    codes_t[...] = values.T.astype(BF)

    stacked = jnp.concatenate(
        [codes[:, s * LAT_TILE : (s + 1) * LAT_TILE] for s in range(CAP)], axis=0
    )
    size = CAP * TILE_ROWS
    row = lax.broadcasted_iota(jnp.int32, (size, size), 0)
    col = lax.broadcasted_iota(jnp.int32, (size, size), 1)
    j, l, c = row // TILE_ROWS, (row % TILE_ROWS) // CAP, row % CAP
    pick = (col == c * TILE_ROWS + 4 * l + j).astype(F32).astype(BF)
    slabs = jnp.dot(pick, stacked, preferred_element_type=F32)
    packed = jnp.concatenate(
        [slabs[s * TILE_ROWS : (s + 1) * TILE_ROWS] for s in range(4)], axis=1
    )
    tile_send[...] = packed.reshape(32, 1, CAP, 4 * LAT_TILE).astype(BF)

    core0 = where[33] == 0
    for n in range(0, WIDTH, step):
        block = jnp.concatenate([t[:, n : n + step] for t in tiles], axis=0)
        part = jnp.dot(codes, block, preferred_element_type=F32)
        for p in range(0, step, 2 * PIECE):
            first = part[:, p : p + PIECE]
            second = part[:, p + PIECE : p + 2 * PIECE]
            at = (n + p) // (2 * PIECE)
            mine[at] = jnp.where(core0, first, second).astype(BF)
            other[at] = jnp.where(core0, second, first).astype(BF)


def encode(ids, counts, where, pieces, dictionary, enc_bias, dec_bias):
    def rows(shape, index):
        return pl.BlockSpec(shape, index)

    piece_spec = rows((4, TILE_ROWS, PIECE), lambda b, *_: (0, b, 0))
    tile_specs = [
        rows((LAT_TILE, WIDTH), lambda b, i, n, w, s=s: (i[b, s], 0)) for s in range(CAP)
    ]
    whole = lambda b, *_: (0, 0)
    return pl.pallas_call(
        encode_kernel,
        grid_spec=pltpu.PrefetchScalarGridSpec(
            num_scalar_prefetch=3,
            grid=(4,),
            in_specs=[piece_spec] * 8
            + tile_specs
            + [rows((32, LAT_TILE), whole), rows((1, WIDTH), whole)],
            out_specs=[
                rows((CAP * LAT_TILE, TILE_ROWS), lambda b, *_: (b, 0)),
                rows((32, 1, CAP, 4 * LAT_TILE), lambda b, *_: (0, b, 0, 0)),
                rows((16, TILE_ROWS, PIECE), lambda b, *_: (0, b, 0)),
                rows((16, TILE_ROWS, PIECE), lambda b, *_: (0, b, 0)),
                rows((TILE_ROWS, PIECE), lambda b, *_: (b, 0)),
            ],
            scratch_shapes=[pltpu.VMEM((TILE_ROWS, WIDTH), BF)],
        ),
        out_shape=[
            jax.ShapeDtypeStruct((4 * CAP * LAT_TILE, TILE_ROWS), BF),
            jax.ShapeDtypeStruct((32, 4, CAP, 4 * LAT_TILE), BF),
            jax.ShapeDtypeStruct((16, ROWS, PIECE), BF),
            jax.ShapeDtypeStruct((16, ROWS, PIECE), BF),
            jax.ShapeDtypeStruct((ROWS, PIECE), BF),
        ],
        compiler_params=params(40),
        cost_estimate=pl.CostEstimate(
            flops=4 * 10**9, bytes_accessed=20 << 20, transcendentals=0
        ),
        name="encode",
    )(ids, counts, where, *pieces, *([dictionary] * CAP), enc_bias, dec_bias)


def first_sum_kernel(table, *refs):
    for k in range(3):
        a, b, out = refs[k], refs[3 + k], refs[6 + k]
        out[...] = (a[...].astype(F32) + b[...].astype(F32)).astype(BF)


def first_sum(table, mine, got):
    specs = [
        pl.BlockSpec((1, ROWS, PIECE), lambda e, tab, k=k: (tab[4 * k + e], 0, 0))
        for k in range(1, 4)
    ]
    return pl.pallas_call(
        first_sum_kernel,
        grid_spec=pltpu.PrefetchScalarGridSpec(
            num_scalar_prefetch=1,
            grid=(4,),
            in_specs=specs + specs,
            out_specs=[pl.BlockSpec((1, ROWS, PIECE), lambda e, tab: (e, 0, 0))] * 3,
        ),
        out_shape=[jax.ShapeDtypeStruct((4, ROWS, PIECE), BF)] * 3,
        compiler_params=params(16),
        name="first_sum",
    )(table, *([mine] * 3), *([got] * 3))


def second_sum_kernel(table, *refs):
    far = refs[6:9]
    for k in range(3):
        total = refs[k][0].astype(F32) + refs[3 + k][0].astype(F32)
        for ref in far:
            total += ref[k + 1].astype(F32)
        refs[9 + k][...] = total.astype(BF)


def second_sum(table, mine, got, far):
    half = ROWS // 2
    specs = [
        pl.BlockSpec((1, half, PIECE), lambda i, tab, e=e: (tab[e], i, 0)) for e in range(1, 4)
    ]
    return pl.pallas_call(
        second_sum_kernel,
        grid_spec=pltpu.PrefetchScalarGridSpec(
            num_scalar_prefetch=1,
            grid=(2,),
            in_specs=specs
            + specs
            + [pl.BlockSpec((4, half, PIECE), lambda i, tab: (0, i, 0))] * 3,
            out_specs=[pl.BlockSpec((half, PIECE), lambda i, tab: (i, 0))] * 3,
        ),
        out_shape=[jax.ShapeDtypeStruct((ROWS, PIECE), BF)] * 3,
        compiler_params=params(16),
        name="second_sum",
    )(table, *([mine] * 3), *([got] * 3), *far)


def error_kernel(table, *refs):
    dec_bias, resid, out, error = refs[8:]
    total = refs[0][0].astype(F32) + refs[1][0].astype(F32)
    for ref in refs[2:5]:
        total += ref[0].astype(F32)
    for ref in refs[5:8]:
        total += ref[...].astype(F32)
    total += dec_bias[...]
    out[...] = total.astype(BF)
    error[...] = (total - resid[...].astype(F32)).astype(BF)


def error_of(table, mine, got, far, near, dec_bias, resid):
    piece = pl.BlockSpec((ROWS, PIECE), lambda i, tab: (0, 0))
    own = pl.BlockSpec((1, ROWS, PIECE), lambda i, tab: (tab[0], 0, 0))
    return pl.pallas_call(
        error_kernel,
        grid_spec=pltpu.PrefetchScalarGridSpec(
            num_scalar_prefetch=1,
            grid=(1,),
            in_specs=[own, own]
            + [pl.BlockSpec((1, ROWS, PIECE), lambda i, tab: (0, 0, 0))] * 3
            + [piece] * 3
            + [pl.BlockSpec((1, PIECE), lambda i, tab: (0, tab[16])), piece],
            out_specs=[piece, piece],
        ),
        out_shape=[jax.ShapeDtypeStruct((ROWS, PIECE), BF)] * 2,
        compiler_params=params(16),
        name="error",
    )(table, mine, got, *far, *near, dec_bias, resid)


def grad_kernel(ids, where, *refs):
    pieces, codes = refs[:8], refs[8:12]
    out, error = refs[12:]

    @pl.when(pl.program_id(0) == 0)
    def _():
        for k in range(8):
            for e in range(4):
                at = k * 4 + e
                row = pl.multiple_of(where[2 * at] * ROWS, ROWS)
                col = where[2 * at + 1]
                error[col // 2, pl.ds(row, ROWS), pl.ds(pl.multiple_of(col % 2 * PIECE, PIECE), PIECE)] = pieces[k][e]

    n = pl.program_id(0)
    out[...] = jnp.zeros_like(out)
    for k, shift in enumerate(SHIFTS):
        for b in range(4):
            row = shift * ROWS + b * TILE_ROWS
            part = jnp.dot(
                codes[k][b * 256 : (b + 1) * 256, :],
                error[n, row : row + TILE_ROWS, :],
                preferred_element_type=F32,
            )
            for s in range(CAP):
                at = pl.multiple_of(ids[k * 16 + b * 4 + s] * LAT_TILE, LAT_TILE)
                out[pl.ds(at, LAT_TILE), :] += part[s * LAT_TILE : (s + 1) * LAT_TILE, :]


def grad(ids, where, pieces, codes):
    width = 2 * PIECE
    return pl.pallas_call(
        grad_kernel,
        grid_spec=pltpu.PrefetchScalarGridSpec(
            num_scalar_prefetch=2,
            grid=(4,),
            in_specs=[pl.BlockSpec((4, ROWS, PIECE), lambda n, *_: (0, 0, 0))] * 8
            + [pl.BlockSpec((4 * CAP * LAT_TILE, TILE_ROWS), lambda n, *_: (0, 0))] * 4,
            out_specs=pl.BlockSpec((2048, width), lambda n, *_: (0, n)),
            scratch_shapes=[pltpu.VMEM((4, 4 * ROWS, width), BF)],
        ),
        out_shape=jax.ShapeDtypeStruct((2048, 1024), F32),
        compiler_params=params(40),
        cost_estimate=pl.CostEstimate(
            flops=10**9, bytes_accessed=14 << 20, transcendentals=0
        ),
        name="grad",
    )(ids, where, *pieces, *codes)


def body(residuals, dictionary, enc_bias, dec_bias, tile_ids, tile_counts):
    t = lax.axis_index("tok")
    lat = lax.axis_index("lat")
    y, x, c = lat // 8, (lat // 2) % SIDE, lat % 2
    shifts = jnp.array(SHIFTS, jnp.int32)

    from_core = jnp.stack([c, 1 - c])[:, None, None]
    far, near = shifts[None, :, None], shifts[None, None, :]
    from_y = (y - jnp.where(from_core == 0, near, far)) % SIDE
    from_x = (x - jnp.where(from_core == 0, far, near)) % SIDE
    lat_from = (from_y * 8 + from_x * 2 + from_core).reshape(32)
    slot = jnp.array([0, 2, 3, 1], jnp.int32)[t]
    own_slot = jnp.where(c == 0, slot, 4 * slot)
    where = jnp.concatenate([lat_from, own_slot[None], c[None]]).astype(jnp.int32)
    grad_where = jnp.stack(
        [
            jnp.broadcast_to(from_y, (2, 4, 4)).reshape(32),
            (from_x * 2 + from_core).reshape(32),
        ],
        axis=1,
    ).reshape(64)
    to_y = jnp.where(c == 0, y + shifts[None, :], y + shifts[:, None])
    to_x = jnp.where(c == 0, x + shifts[:, None], x + shifts[None, :])
    table = (((to_y + t) % SIDE) * 4 + to_x % SIDE).reshape(16)
    own_lat = ((y + t) % SIDE) * 8 + x * 2 + c
    table = jnp.concatenate([table, own_lat[None]]).astype(jnp.int32)

    ids = tile_ids[:, 0, :]
    all_ids = lax.all_gather(ids, "tok", axis=0, tiled=False)
    ids_by_slot = jnp.concatenate(
        [lax.dynamic_index_in_dim(all_ids, (t - s) % SIDE, 0, True) for s in SHIFTS]
    ).reshape(64)

    pieces = gather_plane(residuals)
    codes_t, tile_send, mine, other, resid = encode(
        ids,
        tile_counts[:, 0],
        where,
        pieces,
        dictionary,
        enc_bias.reshape(32, LAT_TILE),
        dec_bias.reshape(1, WIDTH),
    )
    got = send(other, CORE)
    tile_got = lax.all_to_all(tile_send, "lat", split_axis=0, concat_axis=0, tiled=True)
    tile_codes = tile_got.transpose(1, 0, 2, 3)
    codes = [codes_t] + [
        lax.ppermute(codes_t, "tok", [(z, (z + s) % SIDE) for z in range(SIDE)])
        for s in SHIFTS[1:]
    ]

    lines = first_sum(table, mine, got)
    far_in = [send(v, long_leg(d)) for v, d in zip(lines, SHIFTS[1:])]
    parts = second_sum(table, mine, got, far_in)
    near_in = [send(v, short_leg(d)) for v, d in zip(parts, SHIFTS[1:])]
    recon, error = error_of(
        table, mine, got, far_in, near_in, dec_bias.reshape(1, WIDTH), resid
    )
    error = lax.ppermute(error, ("tok", "lat"), TO_PLANE)
    reconstruction = lax.ppermute(recon, ("tok", "lat"), TO_HOME)
    errors = gather_plane(error)
    decoder_grad = grad(ids_by_slot, grad_where, errors, codes)
    return (tile_codes, reconstruction, decoder_grad)


def solution(mesh):
    placed = (
        P("tok", "lat"),
        P("lat", None),
        P("lat"),
        P(),
        P("tok", "lat", None),
        P("tok", "lat"),
    )
    return jax.shard_map(
        body,
        mesh=mesh,
        in_specs=placed,
        out_specs=(P("tok", None, None, "lat"), P("tok", "lat"), P("lat", "tok")),
        check_vma=False,
    )
```

```python
import functools

import jax
import jax.numpy as jnp
import numpy as np
from jax import lax
from jax.experimental import pallas as pl
from jax.experimental.pallas import tpu as pltpu
from jax.sharding import PartitionSpec as P

TILE_ROWS = 128
LAT_TILE = 64
CAP = 4
SIDE = 4
ROWS = 512
WIDTH = 4096
PIECE = 128
SHIFTS = (0, 2, 1, 3)
PARTS = 1
HALF = ROWS // PARTS
BF = jnp.bfloat16
F32 = jnp.float32


def lat_of(y, x, c):
    return (y % SIDE) * 8 + (x % SIDE) * 2 + c


def chips():
    return [(y, x, c) for y in range(SIDE) for x in range(SIDE) for c in range(2)]


def short_leg(d):
    return [
        (lat_of(y, x, c), lat_of(y + d, x, c) if c == 0 else lat_of(y, x + d, c))
        for y, x, c in chips()
    ]


def long_leg(d):
    return [
        (lat_of(y, x, c), lat_of(y, x + d, c) if c == 0 else lat_of(y + d, x, c))
        for y, x, c in chips()
    ]


CORE = [(lat_of(y, x, c), lat_of(y, x, 1 - c)) for y, x, c in chips()]


def plane_leg(d):
    return [
        (z * 32 + a, (z + a // 8) % SIDE * 32 + b) for z in range(SIDE) for a, b in short_leg(d)
    ]


TO_HOME = [
    (z * 32 + lat_of(y, x, c), z * 32 + lat_of(y + z, x, c))
    for z in range(SIDE)
    for y, x, c in chips()
]


def place_table():
    rows = []
    for z in range(SIDE):
        for y, x, c in chips():
            from_lat, at = [], []
            for core in (c, 1 - c):
                for far in SHIFTS:
                    for near in SHIFTS:
                        fy = (y - (near if core == 0 else far)) % SIDE
                        fx = (x - (far if core == 0 else near)) % SIDE
                        from_lat.append(lat_of(fy, fx, core))
                        at += [fy, fx * 2 + core]
            slot = SHIFTS.index((-z) % SIDE)
            sums = []
            for far in SHIFTS:
                for near in SHIFTS:
                    ty = y + (near if c == 0 else far)
                    tx = x + (far if c == 0 else near)
                    sums.append((ty + z) % SIDE * SIDE + tx % SIDE)
            sums.append(lat_of(y + z, x, c))
            rows.append(from_lat + [slot if c == 0 else 4 * slot, c] + at + sums)
    return np.array(rows, np.int32)


def pick_matrix():
    row = np.arange(CAP * TILE_ROWS)
    j, l, c = row // TILE_ROWS, row % TILE_ROWS // CAP, row % CAP
    pick = np.zeros((row.size, row.size), np.float32)
    pick[row, c * TILE_ROWS + 4 * l + j] = 1.0
    return pick


def send(value, pairs):
    return lax.ppermute(value, "lat", pairs)


ANY = pl.BlockSpec(memory_space=pltpu.HBM)
LARGE = pltpu.CompilerParams(vmem_limit_bytes=40 << 20)
SMALL = pltpu.CompilerParams(vmem_limit_bytes=16 << 20)
PLACES = (34, 98)


def stack_kernel(*refs):
    for k in range(4):
        refs[-1][k] = refs[k][...]


def stack4(parts, after):
    shape = parts[0].shape
    whole = pl.BlockSpec(memory_space=pltpu.VMEM)
    return pl.pallas_call(
        stack_kernel,
        in_specs=[whole] * 4 + [ANY] * len(after),
        out_specs=whole,
        out_shape=jax.ShapeDtypeStruct((4,) + shape, BF),
        compiler_params=SMALL,
        name="stack4",
    )(*parts, *after)


def short_gather(piece):
    return [piece] + [send(piece, short_leg(d)) for d in SHIFTS[1:]]


def long_gather(line):
    mine = [line] + [send(line, long_leg(d)) for d in SHIFTS[1:]]
    return mine + [send(v, CORE) for v in mine]


def encode_kernel(first, ids, counts, where, *refs):
    pieces = refs[:8]
    tiles = refs[8:12]
    enc_bias, dec_bias = refs[12:14]
    codes_out, mine, other, resid, centered = refs[-5:]
    b = first + pl.program_id(0)
    for k in range(8):
        for e in range(4):
            slot = k * 4 + e
            off = pl.multiple_of(where[slot] * PIECE, PIECE)
            raw = pieces[k][e]
            centered[:, pl.ds(off, PIECE)] = (
                raw.astype(F32) - dec_bias[:, pl.ds(off, PIECE)]
            ).astype(BF)
            if k == 0 or (k < 4 and e == 0):

                @pl.when(where[32] == slot)
                def _():
                    resid[...] = raw

    step = 512
    preact = jnp.zeros((TILE_ROWS, CAP * LAT_TILE), F32)
    for k in range(0, WIDTH, step):
        block = jnp.concatenate([t[:, k : k + step] for t in tiles], axis=0)
        preact += lax.dot_general(
            centered[:, k : k + step],
            block,
            (((1,), (1,)), ((), ())),
            preferred_element_type=F32,
        )
    bias = jnp.concatenate(
        [enc_bias[pl.ds(ids[b, s], 1), :] for s in range(CAP)], axis=1
    )
    slot_of = lax.broadcasted_iota(jnp.int32, (TILE_ROWS, CAP * LAT_TILE), 1) // LAT_TILE
    live = slot_of < counts[b]
    values = jnp.where(live, jnp.maximum(preact + bias, 0.0), 0.0)
    codes = values.astype(BF)
    codes_out[...] = codes

    core0 = where[33] == 0
    for n in range(0, WIDTH, step):
        block = jnp.concatenate([t[:, n : n + step] for t in tiles], axis=0)
        part = jnp.dot(codes, block, preferred_element_type=F32)
        for p in range(0, step, 2 * PIECE):
            first = part[:, p : p + PIECE]
            second = part[:, p + PIECE : p + 2 * PIECE]
            at = (n + p) // (2 * PIECE)
            mine[at] = jnp.where(core0, first, second).astype(BF)
            other[at] = jnp.where(core0, second, first).astype(BF)


def encode(first, ids, counts, places, pieces, dictionary, enc_bias, dec_bias, after):
    rows = pieces[0].shape[1]
    piece_spec = pl.BlockSpec((4, TILE_ROWS, PIECE), lambda b, *_: (0, b, 0))
    tile_specs = [
        pl.BlockSpec((LAT_TILE, WIDTH), lambda b, i, n, w, s=s: (i[first + b, s], 0))
        for s in range(CAP)
    ]
    whole = lambda b, *_: (0, 0)
    return pl.pallas_call(
        functools.partial(encode_kernel, first),
        grid_spec=pltpu.PrefetchScalarGridSpec(
            num_scalar_prefetch=3,
            grid=(rows // TILE_ROWS,),
            in_specs=[piece_spec] * 8
            + tile_specs
            + [pl.BlockSpec((32, LAT_TILE), whole), pl.BlockSpec((1, WIDTH), whole)]
            + [ANY] * len(after),
            out_specs=[
                pl.BlockSpec((TILE_ROWS, CAP * LAT_TILE), lambda b, *_: (b, 0)),
                pl.BlockSpec((16, TILE_ROWS, PIECE), lambda b, *_: (0, b, 0)),
                pl.BlockSpec((16, TILE_ROWS, PIECE), lambda b, *_: (0, b, 0)),
                pl.BlockSpec((TILE_ROWS, PIECE), lambda b, *_: (b, 0)),
            ],
            scratch_shapes=[pltpu.VMEM((TILE_ROWS, WIDTH), BF)],
        ),
        out_shape=[
            jax.ShapeDtypeStruct((rows, CAP * LAT_TILE), BF),
            jax.ShapeDtypeStruct((16, rows, PIECE), BF),
            jax.ShapeDtypeStruct((16, rows, PIECE), BF),
            jax.ShapeDtypeStruct((rows, PIECE), BF),
        ],
        compiler_params=LARGE,
        cost_estimate=pl.CostEstimate(
            flops=rows << 23, bytes_accessed=rows << 15, transcendentals=0
        ),
        name="encode",
    )(ids, counts, places, *pieces, *([dictionary] * CAP), enc_bias, dec_bias, *after)


def turn_kernel(*refs):
    codes_t = refs[-1]
    ids = refs[PARTS]
    size = CAP * LAT_TILE
    for b in range(4):
        at = b * TILE_ROWS
        codes = refs[at // HALF][at % HALF : at % HALF + TILE_ROWS, :]
        codes_t[b * size : (b + 1) * size, :] = codes.astype(F32).T.astype(BF)
    codes_t[4 * size :, :] = ids[...]


def turn(codes, ids, after):
    id_rows = jnp.zeros((16, TILE_ROWS), BF).at[0, :16].set(ids.reshape(16).astype(BF))
    whole = pl.BlockSpec(memory_space=pltpu.VMEM)
    return pl.pallas_call(
        turn_kernel,
        in_specs=[whole] * (PARTS + 1) + [ANY] * len(after),
        out_specs=whole,
        out_shape=jax.ShapeDtypeStruct((4 * CAP * LAT_TILE + 16, TILE_ROWS), BF),
        compiler_params=SMALL,
        name="turn",
    )(*codes, id_rows, *after)


def pack_kernel(*refs):
    pick, tile_send = refs[PARTS], refs[-1]
    for b in range(4):
        at = b * TILE_ROWS
        codes = refs[at // HALF][at % HALF : at % HALF + TILE_ROWS, :]
        stacked = jnp.concatenate(
            [codes[:, s * LAT_TILE : (s + 1) * LAT_TILE] for s in range(CAP)], axis=0
        )
        slabs = jnp.dot(pick[...], stacked, preferred_element_type=F32)
        packed = jnp.concatenate(
            [slabs[s * TILE_ROWS : (s + 1) * TILE_ROWS] for s in range(4)], axis=1
        )
        tile_send[:, b] = packed.reshape(32, CAP, 4 * LAT_TILE).astype(BF)


def pack(codes, after):
    whole = pl.BlockSpec(memory_space=pltpu.VMEM)
    return pl.pallas_call(
        pack_kernel,
        in_specs=[whole] * (PARTS + 1) + [ANY] * len(after),
        out_specs=whole,
        out_shape=jax.ShapeDtypeStruct((32, 4, CAP, 4 * LAT_TILE), BF),
        compiler_params=SMALL,
        name="pack",
    )(*codes, jnp.asarray(pick_matrix(), BF), *after)


def first_sum_kernel(table, *refs):
    for k in range(3):
        a, b, out = refs[k], refs[3 + k], refs[k - 3]
        out[...] = (a[...].astype(F32) + b[...].astype(F32)).astype(BF)


def first_sum(places, mine, got, after):
    rows = mine.shape[1]
    specs = [
        pl.BlockSpec((1, rows, PIECE), lambda e, p, k=k: (p[PLACES[1] + 4 * k + e], 0, 0))
        for k in range(1, 4)
    ]
    return pl.pallas_call(
        first_sum_kernel,
        grid_spec=pltpu.PrefetchScalarGridSpec(
            num_scalar_prefetch=1,
            grid=(4,),
            in_specs=specs + specs + [ANY] * len(after),
            out_specs=[pl.BlockSpec((1, rows, PIECE), lambda e, p: (e, 0, 0))] * 3,
        ),
        out_shape=[jax.ShapeDtypeStruct((4, rows, PIECE), BF)] * 3,
        compiler_params=LARGE,
        name="first_sum",
    )(places, *([mine] * 3), *([got] * 3), *after)


def second_sum_kernel(table, *refs):
    far = refs[6:9]
    outs = refs[-3:]
    for k in range(3):
        total = refs[k][0].astype(F32) + refs[3 + k][0].astype(F32)
        for ref in far:
            total += ref[k + 1].astype(F32)
        outs[k][...] = total.astype(BF)


def second_sum(places, mine, got, far, after):
    rows = mine.shape[1]
    half = rows // 2
    specs = [
        pl.BlockSpec((1, half, PIECE), lambda i, p, e=e: (p[PLACES[1] + e], i, 0))
        for e in range(1, 4)
    ]
    return pl.pallas_call(
        second_sum_kernel,
        grid_spec=pltpu.PrefetchScalarGridSpec(
            num_scalar_prefetch=1,
            grid=(2,),
            in_specs=specs
            + specs
            + [pl.BlockSpec((4, half, PIECE), lambda i, p: (0, i, 0))] * 3
            + [ANY] * len(after),
            out_specs=[pl.BlockSpec((half, PIECE), lambda i, p: (i, 0))] * 3,
        ),
        out_shape=[jax.ShapeDtypeStruct((rows, PIECE), BF)] * 3,
        compiler_params=LARGE,
        name="second_sum",
    )(places, *([mine] * 3), *([got] * 3), *far, *after)


def error_kernel(table, *refs):
    dec_bias, resid = refs[8:10]
    out, error = refs[-2:]
    total = refs[0][0].astype(F32) + refs[1][0].astype(F32)
    for ref in refs[2:5]:
        total += ref[0].astype(F32)
    for ref in refs[5:8]:
        total += ref[...].astype(F32)
    total += dec_bias[...]
    out[...] = total.astype(BF)
    error[...] = (total - resid[...].astype(F32)).astype(BF)


def error_of(places, mine, got, far, near, dec_bias, resid, after):
    rows = mine.shape[1]
    piece = pl.BlockSpec((rows, PIECE), lambda i, p: (0, 0))
    own = pl.BlockSpec((1, rows, PIECE), lambda i, p: (p[PLACES[1]], 0, 0))
    return pl.pallas_call(
        error_kernel,
        grid_spec=pltpu.PrefetchScalarGridSpec(
            num_scalar_prefetch=1,
            grid=(1,),
            in_specs=[own, own]
            + [pl.BlockSpec((1, rows, PIECE), lambda i, p: (0, 0, 0))] * 3
            + [piece] * 3
            + [pl.BlockSpec((1, PIECE), lambda i, p: (0, p[PLACES[1] + 16])), piece]
            + [ANY] * len(after),
            out_specs=[piece, piece],
        ),
        out_shape=[jax.ShapeDtypeStruct((rows, PIECE), BF)] * 2,
        compiler_params=LARGE,
        name="error",
    )(places, mine, got, *far, *near, dec_bias, resid, *after)


def grad_kernel(ids, places, *refs):
    pieces, codes = refs[: 8 * PARTS], refs[8 * PARTS : 8 * PARTS + 4]
    out, error = refs[-2:]
    n = pl.program_id(0)

    @pl.when(n == 0)
    def _():
        for h in range(PARTS):
            for k in range(8):
                for e in range(4):
                    at = PLACES[0] + 2 * (k * 4 + e)
                    row = pl.multiple_of(places[at] * ROWS + h * HALF, HALF)
                    col = places[at + 1]
                    lane = pl.multiple_of(col % 2 * PIECE, PIECE)
                    error[col // 2, pl.ds(row, HALF), pl.ds(lane, PIECE)] = pieces[8 * h + k][e]

    out[...] = jnp.zeros_like(out)
    for k, shift in enumerate(SHIFTS):
        for b in range(4):
            row = shift * ROWS + b * TILE_ROWS
            part = jnp.dot(
                codes[k][b * 256 : (b + 1) * 256, :],
                error[n, row : row + TILE_ROWS, :],
                preferred_element_type=F32,
            )
            for s in range(CAP):
                at = pl.multiple_of(ids[k * 16 + b * 4 + s] * LAT_TILE, LAT_TILE)
                out[pl.ds(at, LAT_TILE), :] += part[s * LAT_TILE : (s + 1) * LAT_TILE, :]


def grad(ids, places, pieces, codes, after):
    width = 2 * PIECE
    return pl.pallas_call(
        grad_kernel,
        grid_spec=pltpu.PrefetchScalarGridSpec(
            num_scalar_prefetch=2,
            grid=(4,),
            in_specs=[pl.BlockSpec((4, HALF, PIECE), lambda n, *_: (0, 0, 0))] * (8 * PARTS)
            + [pl.BlockSpec((4 * CAP * LAT_TILE + 16, TILE_ROWS), lambda n, *_: (0, 0))] * 4
            + [ANY] * len(after),
            out_specs=pl.BlockSpec((2048, width), lambda n, *_: (0, n)),
            scratch_shapes=[pltpu.VMEM((4, 4 * ROWS, width), BF)],
        ),
        out_shape=jax.ShapeDtypeStruct((2048, 1024), F32),
        compiler_params=LARGE,
        cost_estimate=pl.CostEstimate(
            flops=10**9, bytes_accessed=14 << 20, transcendentals=0
        ),
        name="grad",
    )(ids, places, *pieces, *codes, *after)


def body(residuals, dictionary, enc_bias, dec_bias, tile_ids, tile_counts):
    device = lax.axis_index("tok") * 32 + lax.axis_index("lat")
    places = lax.dynamic_index_in_dim(jnp.asarray(place_table()), device, 0, False)
    ids = tile_ids[:, 0, :]
    counts = tile_counts[:, 0]
    enc_rows = enc_bias.reshape(32, LAT_TILE)
    dec_row = dec_bias.reshape(1, WIDTH)
    halves = range(PARTS)

    near = [short_gather(residuals[h * HALF : (h + 1) * HALF]) for h in halves]
    lines = []
    for h in halves:
        lines.append(stack4(near[h], [enc_rows, places] if h == 0 else [lines[-1]]))
    pieces = [long_gather(lines[h]) for h in halves]

    codes, mine, got, resid, sums = [], [], [], [], []
    for h in halves:
        c, m, o, r = encode(
            h * HALF // TILE_ROWS, ids, counts, places, pieces[h], dictionary,
            enc_rows, dec_row, sums[-1][:1] if sums else [],
        )
        codes.append(c), mine.append(m), resid.append(r)
        got.append(send(o, CORE))
        sums.append(first_sum(places, mine[h], got[h], []))
    far = [[send(v, long_leg(d)) for v, d in zip(sums[h], SHIFTS[1:])] for h in halves]

    codes_t = turn(codes, ids, [])
    all_codes = [codes_t] + [
        lax.ppermute(codes_t, "tok", [(z, (z + s) % SIDE) for z in range(SIDE)])
        for s in SHIFTS[1:]
    ]
    all_ids = jnp.concatenate([v[4 * CAP * LAT_TILE, :16] for v in all_codes]).astype(jnp.int32)
    tile_send = pack(codes, [sums[-1][0], codes_t])
    tile_got = lax.all_to_all(tile_send, "lat", split_axis=0, concat_axis=0, tiled=True)
    tile_codes = tile_got.transpose(1, 0, 2, 3)

    recon, error = [], []
    parts = []
    last = tile_send
    for h in halves:
        parts.append(second_sum(places, mine[h], got[h], far[h], [last]))
        last = parts[h][0]
    for h in halves:
        back = [send(v, short_leg(d)) for v, d in zip(parts[h], SHIFTS[1:])]
        r, e = error_of(
            places, mine[h], got[h], far[h], back, dec_row, resid[h],
            [last] if h else [last, all_ids, tile_got],
        )
        last = r
        recon.append(r)
        error.append(e)
    whole = recon[0] if PARTS == 1 else jnp.concatenate(recon)
    reconstruction = lax.ppermute(whole, ("tok", "lat"), TO_HOME)
    last = reconstruction
    error_lines = []
    for h in halves:
        legs = [lax.ppermute(error[h], ("tok", "lat"), plane_leg(d)) for d in SHIFTS]
        error_lines.append(stack4(legs, [last]))
        last = error_lines[h]
    errors = [long_gather(error_lines[h]) for h in halves]
    decoder_grad = grad(all_ids, places, sum(errors, []), all_codes, [])
    return (tile_codes, reconstruction, decoder_grad)


def solution(mesh):
    placed = (
        P("tok", "lat"),
        P("lat", None),
        P("lat"),
        P(),
        P("tok", "lat", None),
        P("tok", "lat"),
    )
    return jax.shard_map(
        body,
        mesh=mesh,
        in_specs=placed,
        out_specs=(P("tok", None, None, "lat"), P("tok", "lat"), P("lat", "tok")),
        check_vma=False,
    )
```

```python
import functools

import jax
import jax.numpy as jnp
import numpy as np
from jax import lax
from jax.experimental import pallas as pl
from jax.experimental.pallas import tpu as pltpu
from jax.sharding import PartitionSpec as P

TILE_ROWS = 128
LAT_TILE = 64
CAP = 4
SIDE = 4
ROWS = 512
WIDTH = 4096
PIECE = 128
SHIFTS = (0, 2, 1, 3)
PARTS = 1
HALF = ROWS // PARTS
BF = jnp.bfloat16
F32 = jnp.float32


def lat_of(y, x, c):
    return (y % SIDE) * 8 + (x % SIDE) * 2 + c


def chips():
    return [(y, x, c) for y in range(SIDE) for x in range(SIDE) for c in range(2)]


def short_leg(d):
    return [
        (lat_of(y, x, c), lat_of(y + d, x, c) if c == 0 else lat_of(y, x + d, c))
        for y, x, c in chips()
    ]


def long_leg(d):
    return [
        (lat_of(y, x, c), lat_of(y, x + d, c) if c == 0 else lat_of(y + d, x, c))
        for y, x, c in chips()
    ]


CORE = [(lat_of(y, x, c), lat_of(y, x, 1 - c)) for y, x, c in chips()]


def plane_leg(d):
    return [
        (z * 32 + a, (z + a // 8) % SIDE * 32 + b) for z in range(SIDE) for a, b in short_leg(d)
    ]


TO_HOME = [
    (z * 32 + lat_of(y, x, c), z * 32 + lat_of(y + z, x, c))
    for z in range(SIDE)
    for y, x, c in chips()
]


def place_table():
    rows = []
    for z in range(SIDE):
        for y, x, c in chips():
            from_lat, at = [], []
            for core in (c, 1 - c):
                for far in SHIFTS:
                    for near in SHIFTS:
                        fy = (y - (near if core == 0 else far)) % SIDE
                        fx = (x - (far if core == 0 else near)) % SIDE
                        from_lat.append(lat_of(fy, fx, core))
                        at += [fy, fx * 2 + core]
            slot = SHIFTS.index((-z) % SIDE)
            sums = []
            for far in SHIFTS:
                for near in SHIFTS:
                    ty = y + (near if c == 0 else far)
                    tx = x + (far if c == 0 else near)
                    sums.append((ty + z) % SIDE * SIDE + tx % SIDE)
            sums.append(lat_of(y + z, x, c))
            rows.append(from_lat + [slot if c == 0 else 4 * slot, c] + at + sums)
    return np.array(rows, np.int32)


def pick_matrix():
    row = np.arange(CAP * TILE_ROWS)
    j, l, c = row // TILE_ROWS, row % TILE_ROWS // CAP, row % CAP
    pick = np.zeros((row.size, row.size), np.float32)
    pick[row, c * TILE_ROWS + 4 * l + j] = 1.0
    return pick


def send(value, pairs):
    return lax.ppermute(value, "lat", pairs)


ANY = pl.BlockSpec(memory_space=pltpu.HBM)
LARGE = pltpu.CompilerParams(vmem_limit_bytes=40 << 20)
SMALL = pltpu.CompilerParams(vmem_limit_bytes=16 << 20)
PLACES = (34, 98)


def stack_kernel(*refs):
    for k in range(4):
        refs[-1][k] = refs[k][...]


def stack4(parts, after):
    shape = parts[0].shape
    whole = pl.BlockSpec(memory_space=pltpu.VMEM)
    return pl.pallas_call(
        stack_kernel,
        in_specs=[whole] * 4 + [ANY] * len(after),
        out_specs=whole,
        out_shape=jax.ShapeDtypeStruct((4,) + shape, BF),
        compiler_params=SMALL,
        name="stack4",
    )(*parts, *after)


def short_gather(piece):
    return [piece] + [send(piece, short_leg(d)) for d in SHIFTS[1:]]


def long_gather(line):
    mine = [line] + [send(line, long_leg(d)) for d in SHIFTS[1:]]
    return mine + [send(v, CORE) for v in mine]


def add_pieces(total, places, numbers, pieces, tiles, dec_bias):
    for k, ref in zip(numbers, pieces):
        for e in range(0, 4, 2):
            offs = [pl.multiple_of(places[4 * k + e + i] * PIECE, PIECE) for i in range(2)]
            centered = [
                (ref[e + i].astype(F32) - dec_bias[:, pl.ds(offs[i], PIECE)]).astype(BF)
                for i in range(2)
            ]
            block = [
                jnp.concatenate([t[:, pl.ds(offs[i], PIECE)] for t in tiles], axis=0)
                for i in range(2)
            ]
            total += lax.dot_general(
                jnp.concatenate(centered, axis=1),
                jnp.concatenate(block, axis=1),
                (((1,), (1,)), ((), ())),
                preferred_element_type=F32,
            )
    return total


EARLY, LATE = (0, 1, 4), (2, 3, 5, 6, 7)


def begin_kernel(ids, places, *refs):
    pieces, tiles, dec_bias, out = refs[:3], refs[3:7], refs[7], refs[8]
    total = jnp.zeros((TILE_ROWS, CAP * LAT_TILE), F32)
    out[...] = add_pieces(total, places, EARLY, pieces, tiles, dec_bias)


def begin(ids, places, pieces, dictionary, dec_bias):
    return pl.pallas_call(
        begin_kernel,
        grid_spec=pltpu.PrefetchScalarGridSpec(
            num_scalar_prefetch=2,
            grid=(4,),
            in_specs=[pl.BlockSpec((4, TILE_ROWS, PIECE), lambda b, *_: (0, b, 0))] * 3
            + [
                pl.BlockSpec((LAT_TILE, WIDTH), lambda b, i, w, s=s: (i[b, s], 0))
                for s in range(CAP)
            ]
            + [pl.BlockSpec((1, WIDTH), lambda b, *_: (0, 0))],
            out_specs=pl.BlockSpec((TILE_ROWS, CAP * LAT_TILE), lambda b, *_: (b, 0)),
        ),
        out_shape=jax.ShapeDtypeStruct((ROWS, CAP * LAT_TILE), F32),
        compiler_params=LARGE,
        cost_estimate=pl.CostEstimate(
            flops=10**9, bytes_accessed=48 << 20, transcendentals=0
        ),
        name="begin",
    )(ids, places, *pieces, *([dictionary] * CAP), dec_bias)


def encode_kernel(ids, counts, where, *refs):
    pieces = refs[:5]
    own_line, next_line, begun = refs[5:8]
    tiles = refs[8:12]
    enc_bias, dec_bias = refs[12:14]
    codes_out, mine, other, resid = refs[14:]
    b = pl.program_id(0)
    step = 512
    held = [(e, own_line, e) for e in range(4)]
    held += [(4, next_line, 0), (8, pieces[0], 0), (12, pieces[1], 0)]
    for slot, ref, e in held:

        @pl.when(where[32] == slot)
        def _():
            resid[...] = ref[e]

    preact = add_pieces(begun[...], where, LATE, pieces, tiles, dec_bias)
    bias = jnp.concatenate(
        [enc_bias[pl.ds(ids[b, s], 1), :] for s in range(CAP)], axis=1
    )
    slot_of = lax.broadcasted_iota(jnp.int32, (TILE_ROWS, CAP * LAT_TILE), 1) // LAT_TILE
    live = slot_of < counts[b]
    values = jnp.where(live, jnp.maximum(preact + bias, 0.0), 0.0)
    codes = values.astype(BF)
    codes_out[...] = codes

    core0 = where[33] == 0
    for n in range(0, WIDTH, step):
        block = jnp.concatenate([t[:, n : n + step] for t in tiles], axis=0)
        part = jnp.dot(codes, block, preferred_element_type=F32)
        for p in range(0, step, 2 * PIECE):
            first = part[:, p : p + PIECE]
            second = part[:, p + PIECE : p + 2 * PIECE]
            at = (n + p) // (2 * PIECE)
            mine[at] = jnp.where(core0, first, second).astype(BF)
            other[at] = jnp.where(core0, second, first).astype(BF)


def encode(ids, counts, places, pieces, begun, dictionary, enc_bias, dec_bias):
    piece_spec = pl.BlockSpec((4, TILE_ROWS, PIECE), lambda b, *_: (0, b, 0))
    code_spec = pl.BlockSpec((TILE_ROWS, CAP * LAT_TILE), lambda b, *_: (b, 0))
    tile_specs = [
        pl.BlockSpec((LAT_TILE, WIDTH), lambda b, i, n, w, s=s: (i[b, s], 0)) for s in range(CAP)
    ]
    whole = lambda b, *_: (0, 0)
    return pl.pallas_call(
        encode_kernel,
        grid_spec=pltpu.PrefetchScalarGridSpec(
            num_scalar_prefetch=3,
            grid=(4,),
            in_specs=[piece_spec] * 6
            + [pl.BlockSpec((1, TILE_ROWS, PIECE), lambda b, *_: (0, b, 0)), code_spec]
            + tile_specs
            + [pl.BlockSpec((32, LAT_TILE), whole), pl.BlockSpec((1, WIDTH), whole)],
            out_specs=[
                code_spec,
                piece_spec_of(16),
                piece_spec_of(16),
                pl.BlockSpec((TILE_ROWS, PIECE), lambda b, *_: (b, 0)),
            ],
        ),
        out_shape=[
            jax.ShapeDtypeStruct((ROWS, CAP * LAT_TILE), BF),
            jax.ShapeDtypeStruct((16, ROWS, PIECE), BF),
            jax.ShapeDtypeStruct((16, ROWS, PIECE), BF),
            jax.ShapeDtypeStruct((ROWS, PIECE), BF),
        ],
        compiler_params=LARGE,
        name="encode",
    )(
        ids, counts, places, *[pieces[k] for k in LATE], pieces[0], pieces[1], begun,
        *([dictionary] * CAP), enc_bias, dec_bias,
    )


def piece_spec_of(count):
    return pl.BlockSpec((count, TILE_ROWS, PIECE), lambda b, *_: (0, b, 0))


def turn_kernel(*refs):
    codes_t = refs[-1]
    ids = refs[1]
    size = CAP * LAT_TILE
    for b in range(4):
        at = b * TILE_ROWS
        codes = refs[0][at : at + TILE_ROWS, :]
        codes_t[b * size : (b + 1) * size, :] = codes.astype(F32).T.astype(BF)
    codes_t[4 * size :, :] = ids[...]


def turn(codes, ids, after):
    id_rows = jnp.zeros((16, TILE_ROWS), BF).at[0, :16].set(ids.reshape(16).astype(BF))
    whole = pl.BlockSpec(memory_space=pltpu.VMEM)
    return pl.pallas_call(
        turn_kernel,
        in_specs=[whole] * 2 + [ANY] * len(after),
        out_specs=whole,
        out_shape=jax.ShapeDtypeStruct((4 * CAP * LAT_TILE + 16, TILE_ROWS), BF),
        compiler_params=SMALL,
        name="turn",
    )(codes, id_rows, *after)


def pack_kernel(*refs):
    pick, tile_send = refs[1], refs[-1]
    for b in range(4):
        at = b * TILE_ROWS
        codes = refs[0][at : at + TILE_ROWS, :]
        stacked = jnp.concatenate(
            [codes[:, s * LAT_TILE : (s + 1) * LAT_TILE] for s in range(CAP)], axis=0
        )
        slabs = jnp.dot(pick[...], stacked, preferred_element_type=F32)
        packed = jnp.concatenate(
            [slabs[s * TILE_ROWS : (s + 1) * TILE_ROWS] for s in range(4)], axis=1
        )
        tile_send[:, b] = packed.reshape(32, CAP, 4 * LAT_TILE).astype(BF)


def pack(codes, after):
    whole = pl.BlockSpec(memory_space=pltpu.VMEM)
    return pl.pallas_call(
        pack_kernel,
        in_specs=[whole] * 2 + [ANY] * len(after),
        out_specs=whole,
        out_shape=jax.ShapeDtypeStruct((32, 4, CAP, 4 * LAT_TILE), BF),
        compiler_params=SMALL,
        name="pack",
    )(codes, jnp.asarray(pick_matrix(), BF), *after)


def first_sum_kernel(table, *refs):
    for k in range(3):
        a, b, out = refs[k], refs[3 + k], refs[k - 3]
        out[...] = (a[...].astype(F32) + b[...].astype(F32)).astype(BF)


def first_sum(places, mine, got, after):
    rows = mine.shape[1]
    specs = [
        pl.BlockSpec((1, rows, PIECE), lambda e, p, k=k: (p[PLACES[1] + 4 * k + e], 0, 0))
        for k in range(1, 4)
    ]
    return pl.pallas_call(
        first_sum_kernel,
        grid_spec=pltpu.PrefetchScalarGridSpec(
            num_scalar_prefetch=1,
            grid=(4,),
            in_specs=specs + specs + [ANY] * len(after),
            out_specs=[pl.BlockSpec((1, rows, PIECE), lambda e, p: (e, 0, 0))] * 3,
        ),
        out_shape=[jax.ShapeDtypeStruct((4, rows, PIECE), BF)] * 3,
        compiler_params=LARGE,
        name="first_sum",
    )(places, *([mine] * 3), *([got] * 3), *after)


def second_sum_kernel(table, *refs):
    far = refs[6:9]
    outs = refs[-3:]
    for k in range(3):
        total = refs[k][0].astype(F32) + refs[3 + k][0].astype(F32)
        for ref in far:
            total += ref[k + 1].astype(F32)
        outs[k][...] = total.astype(BF)


def second_sum(places, mine, got, far, after):
    rows = mine.shape[1]
    half = rows // 2
    specs = [
        pl.BlockSpec((1, half, PIECE), lambda i, p, e=e: (p[PLACES[1] + e], i, 0))
        for e in range(1, 4)
    ]
    return pl.pallas_call(
        second_sum_kernel,
        grid_spec=pltpu.PrefetchScalarGridSpec(
            num_scalar_prefetch=1,
            grid=(2,),
            in_specs=specs
            + specs
            + [pl.BlockSpec((4, half, PIECE), lambda i, p: (0, i, 0))] * 3
            + [ANY] * len(after),
            out_specs=[pl.BlockSpec((half, PIECE), lambda i, p: (i, 0))] * 3,
        ),
        out_shape=[jax.ShapeDtypeStruct((rows, PIECE), BF)] * 3,
        compiler_params=LARGE,
        name="second_sum",
    )(places, *([mine] * 3), *([got] * 3), *far, *after)


def error_kernel(table, *refs):
    dec_bias, resid = refs[8:10]
    out, error = refs[-2:]
    total = refs[0][0].astype(F32) + refs[1][0].astype(F32)
    for ref in refs[2:5]:
        total += ref[0].astype(F32)
    for ref in refs[5:8]:
        total += ref[...].astype(F32)
    total += dec_bias[...]
    out[...] = total.astype(BF)
    error[...] = (total - resid[...].astype(F32)).astype(BF)


def error_of(places, mine, got, far, near, dec_bias, resid, after):
    rows = mine.shape[1]
    piece = pl.BlockSpec((rows, PIECE), lambda i, p: (0, 0))
    own = pl.BlockSpec((1, rows, PIECE), lambda i, p: (p[PLACES[1]], 0, 0))
    return pl.pallas_call(
        error_kernel,
        grid_spec=pltpu.PrefetchScalarGridSpec(
            num_scalar_prefetch=1,
            grid=(1,),
            in_specs=[own, own]
            + [pl.BlockSpec((1, rows, PIECE), lambda i, p: (0, 0, 0))] * 3
            + [piece] * 3
            + [pl.BlockSpec((1, PIECE), lambda i, p: (0, p[PLACES[1] + 16])), piece]
            + [ANY] * len(after),
            out_specs=[piece, piece],
        ),
        out_shape=[jax.ShapeDtypeStruct((rows, PIECE), BF)] * 2,
        compiler_params=LARGE,
        name="error",
    )(places, mine, got, *far, *near, dec_bias, resid, *after)


def grad_kernel(ids, places, *refs):
    pieces, codes = refs[: 8 * PARTS], refs[8 * PARTS : 8 * PARTS + 4]
    out, error = refs[-2:]
    n = pl.program_id(0)

    @pl.when(n == 0)
    def _():
        for h in range(PARTS):
            for k in range(8):
                for e in range(4):
                    at = PLACES[0] + 2 * (k * 4 + e)
                    row = pl.multiple_of(places[at] * ROWS + h * HALF, HALF)
                    col = places[at + 1]
                    lane = pl.multiple_of(col % 2 * PIECE, PIECE)
                    error[col // 2, pl.ds(row, HALF), pl.ds(lane, PIECE)] = pieces[8 * h + k][e]

    out[...] = jnp.zeros_like(out)
    for k, shift in enumerate(SHIFTS):
        for b in range(4):
            row = shift * ROWS + b * TILE_ROWS
            part = jnp.dot(
                codes[k][b * 256 : (b + 1) * 256, :],
                error[n, row : row + TILE_ROWS, :],
                preferred_element_type=F32,
            )
            for s in range(CAP):
                at = pl.multiple_of(ids[k * 16 + b * 4 + s] * LAT_TILE, LAT_TILE)
                out[pl.ds(at, LAT_TILE), :] += part[s * LAT_TILE : (s + 1) * LAT_TILE, :]


def grad(ids, places, pieces, codes, after):
    width = 2 * PIECE
    return pl.pallas_call(
        grad_kernel,
        grid_spec=pltpu.PrefetchScalarGridSpec(
            num_scalar_prefetch=2,
            grid=(4,),
            in_specs=[pl.BlockSpec((4, HALF, PIECE), lambda n, *_: (0, 0, 0))] * (8 * PARTS)
            + [pl.BlockSpec((4 * CAP * LAT_TILE + 16, TILE_ROWS), lambda n, *_: (0, 0))] * 4
            + [ANY] * len(after),
            out_specs=pl.BlockSpec((2048, width), lambda n, *_: (0, n)),
            scratch_shapes=[pltpu.VMEM((4, 4 * ROWS, width), BF)],
        ),
        out_shape=jax.ShapeDtypeStruct((2048, 1024), F32),
        compiler_params=LARGE,
        cost_estimate=pl.CostEstimate(
            flops=10**9, bytes_accessed=14 << 20, transcendentals=0
        ),
        name="grad",
    )(ids, places, *pieces, *codes, *after)


def body(residuals, dictionary, enc_bias, dec_bias, tile_ids, tile_counts):
    device = lax.axis_index("tok") * 32 + lax.axis_index("lat")
    places = lax.dynamic_index_in_dim(jnp.asarray(place_table()), device, 0, False)
    ids = tile_ids[:, 0, :]
    counts = tile_counts[:, 0]
    enc_rows = enc_bias.reshape(32, LAT_TILE)
    dec_row = dec_bias.reshape(1, WIDTH)
    halves = range(PARTS)

    line = stack4(short_gather(residuals), [enc_rows, places])
    own = [line] + [send(line, long_leg(d)) for d in SHIFTS[1:]]
    swapped = [send(v, CORE) for v in own[:1]]
    begun = begin(ids, places, own[:2] + swapped, dictionary, dec_row)
    own[3], begun = lax.optimization_barrier((own[3], begun))
    pieces = own + swapped + [send(v, CORE) for v in own[1:]]

    codes, m, other, r = encode(
        ids, counts, places, pieces, begun, dictionary, enc_rows, dec_row
    )
    mine, resid = [m], [r]
    got = [send(other, CORE)]
    sums = [first_sum(places, m, got[0], [])]
    far = [[send(v, long_leg(d)) for v, d in zip(sums[0], SHIFTS[1:])]]

    codes_t = turn(codes, ids, [])
    all_codes = [codes_t] + [
        lax.ppermute(codes_t, "tok", [(z, (z + s) % SIDE) for z in range(SIDE)])
        for s in SHIFTS[1:]
    ]
    all_ids = jnp.concatenate([v[4 * CAP * LAT_TILE, :16] for v in all_codes]).astype(jnp.int32)
    tile_send = pack(codes, [sums[-1][0], codes_t])
    tile_got = lax.all_to_all(tile_send, "lat", split_axis=0, concat_axis=0, tiled=True)
    tile_codes = tile_got.transpose(1, 0, 2, 3)

    recon, error = [], []
    parts = []
    last = tile_send
    for h in halves:
        parts.append(second_sum(places, mine[h], got[h], far[h], [last]))
        last = parts[h][0]
    for h in halves:
        back = [send(v, short_leg(d)) for v, d in zip(parts[h], SHIFTS[1:])]
        r, e = error_of(
            places, mine[h], got[h], far[h], back, dec_row, resid[h],
            [last] if h else [last, all_ids, tile_got],
        )
        last = r
        recon.append(r)
        error.append(e)
    whole = recon[0] if PARTS == 1 else jnp.concatenate(recon)
    error_lines = []
    for h in halves:
        legs = [lax.ppermute(error[h], ("tok", "lat"), plane_leg(d)) for d in SHIFTS]
        error_lines.append(stack4(legs, [last]))
        last = error_lines[h]
    line = error_lines[0]
    own = [line] + [send(line, long_leg(d)) for d in SHIFTS[1:]]
    own[1], whole = lax.optimization_barrier((own[1], whole))
    reconstruction = lax.ppermute(whole, ("tok", "lat"), TO_HOME)
    own[3], reconstruction = lax.optimization_barrier((own[3], reconstruction))
    errors = [own + [send(v, CORE) for v in own]]
    decoder_grad = grad(all_ids, places, sum(errors, []), all_codes, [])
    return (tile_codes, reconstruction, decoder_grad)


def solution(mesh):
    placed = (
        P("tok", "lat"),
        P("lat", None),
        P("lat"),
        P(),
        P("tok", "lat", None),
        P("tok", "lat"),
    )
    return jax.shard_map(
        body,
        mesh=mesh,
        in_specs=placed,
        out_specs=(P("tok", None, None, "lat"), P("tok", "lat"), P("lat", "tok")),
        check_vma=False,
    )
```

```python
import functools

import jax
import jax.numpy as jnp
import numpy as np
from jax import lax
from jax.experimental import pallas as pl
from jax.experimental.pallas import tpu as pltpu
from jax.sharding import PartitionSpec as P

TILE_ROWS = 128
LAT_TILE = 64
CAP = 4
SIDE = 4
ROWS = 512
WIDTH = 4096
PIECE = 128
SHIFTS = (0, 2, 1, 3)
PARTS = 1
HALF = ROWS // PARTS
BF = jnp.bfloat16
F32 = jnp.float32


def lat_of(y, x, c):
    return (y % SIDE) * 8 + (x % SIDE) * 2 + c


def chips():
    return [(y, x, c) for y in range(SIDE) for x in range(SIDE) for c in range(2)]


def short_leg(d):
    return [
        (lat_of(y, x, c), lat_of(y + d, x, c) if c == 0 else lat_of(y, x + d, c))
        for y, x, c in chips()
    ]


def long_leg(d):
    return [
        (lat_of(y, x, c), lat_of(y, x + d, c) if c == 0 else lat_of(y + d, x, c))
        for y, x, c in chips()
    ]


CORE = [(lat_of(y, x, c), lat_of(y, x, 1 - c)) for y, x, c in chips()]


def plane_leg(d):
    return [
        (z * 32 + a, (z + a // 8) % SIDE * 32 + b) for z in range(SIDE) for a, b in short_leg(d)
    ]


TO_HOME = [
    (z * 32 + lat_of(y, x, c), z * 32 + lat_of(y + z, x, c))
    for z in range(SIDE)
    for y, x, c in chips()
]


def place_table():
    rows = []
    for z in range(SIDE):
        for y, x, c in chips():
            from_lat, at = [], []
            for core in (c, 1 - c):
                for far in SHIFTS:
                    for near in SHIFTS:
                        fy = (y - (near if core == 0 else far)) % SIDE
                        fx = (x - (far if core == 0 else near)) % SIDE
                        from_lat.append(lat_of(fy, fx, core))
                        at += [fy, fx * 2 + core]
            slot = SHIFTS.index((-z) % SIDE)
            sums = []
            for far in SHIFTS:
                for near in SHIFTS:
                    ty = y + (near if c == 0 else far)
                    tx = x + (far if c == 0 else near)
                    sums.append((ty + z) % SIDE * SIDE + tx % SIDE)
            sums.append(lat_of(y + z, x, c))
            rows.append(from_lat + [slot if c == 0 else 4 * slot, c] + at + sums)
    return np.array(rows, np.int32)


def pick_matrix():
    row = np.arange(CAP * TILE_ROWS)
    j, l, c = row // TILE_ROWS, row % TILE_ROWS // CAP, row % CAP
    pick = np.zeros((row.size, row.size), np.float32)
    pick[row, c * TILE_ROWS + 4 * l + j] = 1.0
    return pick


def send(value, pairs):
    return lax.ppermute(value, "lat", pairs)


ANY = pl.BlockSpec(memory_space=pltpu.HBM)
LARGE = pltpu.CompilerParams(vmem_limit_bytes=40 << 20)
SMALL = pltpu.CompilerParams(vmem_limit_bytes=16 << 20)
PLACES = (34, 98)


def stack_kernel(*refs):
    for k in range(4):
        refs[-1][k] = refs[k][...]


def stack4(parts, after):
    shape = parts[0].shape
    whole = pl.BlockSpec(memory_space=pltpu.VMEM)
    return pl.pallas_call(
        stack_kernel,
        in_specs=[whole] * 4 + [ANY] * len(after),
        out_specs=whole,
        out_shape=jax.ShapeDtypeStruct((4,) + shape, BF),
        compiler_params=SMALL,
        name="stack4",
    )(*parts, *after)


def short_gather(piece):
    return [piece] + [send(piece, short_leg(d)) for d in SHIFTS[1:]]


def long_gather(line):
    mine = [line] + [send(line, long_leg(d)) for d in SHIFTS[1:]]
    return mine + [send(v, CORE) for v in mine]


def add_pieces(total, places, numbers, pieces, tiles, dec_bias):
    for k, ref in zip(numbers, pieces):
        for e in range(0, 4, 2):
            offs = [pl.multiple_of(places[4 * k + e + i] * PIECE, PIECE) for i in range(2)]
            centered = [
                (ref[e + i].astype(F32) - dec_bias[:, pl.ds(offs[i], PIECE)]).astype(BF)
                for i in range(2)
            ]
            block = [
                jnp.concatenate([t[:, pl.ds(offs[i], PIECE)] for t in tiles], axis=0)
                for i in range(2)
            ]
            total += lax.dot_general(
                jnp.concatenate(centered, axis=1),
                jnp.concatenate(block, axis=1),
                (((1,), (1,)), ((), ())),
                preferred_element_type=F32,
            )
    return total


EARLY, LATE = (0, 1, 4), (2, 3, 5, 6, 7)


def begin_kernel(ids, places, *refs):
    pieces, tiles, dec_bias, out = refs[:3], refs[3:7], refs[7], refs[8]
    total = jnp.zeros((TILE_ROWS, CAP * LAT_TILE), F32)
    out[...] = add_pieces(total, places, EARLY, pieces, tiles, dec_bias)


def begin(ids, places, pieces, dictionary, dec_bias):
    return pl.pallas_call(
        begin_kernel,
        grid_spec=pltpu.PrefetchScalarGridSpec(
            num_scalar_prefetch=2,
            grid=(4,),
            in_specs=[pl.BlockSpec((4, TILE_ROWS, PIECE), lambda b, *_: (0, b, 0))] * 3
            + [
                pl.BlockSpec((LAT_TILE, WIDTH), lambda b, i, w, s=s: (i[b, s], 0))
                for s in range(CAP)
            ]
            + [pl.BlockSpec((1, WIDTH), lambda b, *_: (0, 0))],
            out_specs=pl.BlockSpec((TILE_ROWS, CAP * LAT_TILE), lambda b, *_: (b, 0)),
        ),
        out_shape=jax.ShapeDtypeStruct((ROWS, CAP * LAT_TILE), F32),
        compiler_params=LARGE,
        cost_estimate=pl.CostEstimate(
            flops=10**9, bytes_accessed=48 << 20, transcendentals=0
        ),
        name="begin",
    )(ids, places, *pieces, *([dictionary] * CAP), dec_bias)


def encode_kernel(ids, counts, where, *refs):
    pieces = refs[:5]
    own_line, next_line, begun = refs[5:8]
    tiles = refs[8:12]
    enc_bias, dec_bias = refs[12:14]
    codes_out, mine, other, resid = refs[14:]
    b = pl.program_id(0)
    step = 512
    held = [(e, own_line, e) for e in range(4)]
    held += [(4, next_line, 0), (8, pieces[0], 0), (12, pieces[1], 0)]
    for slot, ref, e in held:

        @pl.when(where[32] == slot)
        def _():
            resid[...] = ref[e]

    preact = add_pieces(begun[...], where, LATE, pieces, tiles, dec_bias)
    bias = jnp.concatenate(
        [enc_bias[pl.ds(ids[b, s], 1), :] for s in range(CAP)], axis=1
    )
    slot_of = lax.broadcasted_iota(jnp.int32, (TILE_ROWS, CAP * LAT_TILE), 1) // LAT_TILE
    live = slot_of < counts[b]
    values = jnp.where(live, jnp.maximum(preact + bias, 0.0), 0.0)
    codes = values.astype(BF)
    codes_out[...] = codes

    core0 = where[33] == 0
    for n in range(0, WIDTH, step):
        block = jnp.concatenate([t[:, n : n + step] for t in tiles], axis=0)
        part = jnp.dot(codes, block, preferred_element_type=F32)
        for p in range(0, step, 2 * PIECE):
            first = part[:, p : p + PIECE]
            second = part[:, p + PIECE : p + 2 * PIECE]
            at = (n + p) // (2 * PIECE)
            mine[at] = jnp.where(core0, first, second).astype(BF)
            other[at] = jnp.where(core0, second, first).astype(BF)


def encode(ids, counts, places, pieces, begun, dictionary, enc_bias, dec_bias):
    piece_spec = pl.BlockSpec((4, TILE_ROWS, PIECE), lambda b, *_: (0, b, 0))
    code_spec = pl.BlockSpec((TILE_ROWS, CAP * LAT_TILE), lambda b, *_: (b, 0))
    tile_specs = [
        pl.BlockSpec((LAT_TILE, WIDTH), lambda b, i, n, w, s=s: (i[b, s], 0)) for s in range(CAP)
    ]
    whole = lambda b, *_: (0, 0)
    return pl.pallas_call(
        encode_kernel,
        grid_spec=pltpu.PrefetchScalarGridSpec(
            num_scalar_prefetch=3,
            grid=(4,),
            in_specs=[piece_spec] * 6
            + [pl.BlockSpec((1, TILE_ROWS, PIECE), lambda b, *_: (0, b, 0)), code_spec]
            + tile_specs
            + [pl.BlockSpec((32, LAT_TILE), whole), pl.BlockSpec((1, WIDTH), whole)],
            out_specs=[
                code_spec,
                piece_spec_of(16),
                piece_spec_of(16),
                pl.BlockSpec((TILE_ROWS, PIECE), lambda b, *_: (b, 0)),
            ],
        ),
        out_shape=[
            jax.ShapeDtypeStruct((ROWS, CAP * LAT_TILE), BF),
            jax.ShapeDtypeStruct((16, ROWS, PIECE), BF),
            jax.ShapeDtypeStruct((16, ROWS, PIECE), BF),
            jax.ShapeDtypeStruct((ROWS, PIECE), BF),
        ],
        compiler_params=LARGE,
        name="encode",
    )(
        ids, counts, places, *[pieces[k] for k in LATE], pieces[0], pieces[1], begun,
        *([dictionary] * CAP), enc_bias, dec_bias,
    )


def piece_spec_of(count):
    return pl.BlockSpec((count, TILE_ROWS, PIECE), lambda b, *_: (0, b, 0))


def turn_kernel(*refs):
    codes_t = refs[-1]
    ids = refs[1]
    size = CAP * LAT_TILE
    for b in range(4):
        at = b * TILE_ROWS
        codes = refs[0][at : at + TILE_ROWS, :]
        codes_t[b * size : (b + 1) * size, :] = codes.astype(F32).T.astype(BF)
    codes_t[4 * size :, :] = ids[...]


def turn(codes, ids, after):
    id_rows = jnp.zeros((16, TILE_ROWS), BF).at[0, :16].set(ids.reshape(16).astype(BF))
    whole = pl.BlockSpec(memory_space=pltpu.VMEM)
    return pl.pallas_call(
        turn_kernel,
        in_specs=[whole] * 2 + [ANY] * len(after),
        out_specs=whole,
        out_shape=jax.ShapeDtypeStruct((4 * CAP * LAT_TILE + 16, TILE_ROWS), BF),
        compiler_params=SMALL,
        name="turn",
    )(codes, id_rows, *after)


def pack_kernel(*refs):
    pick, tile_send = refs[1], refs[-1]
    for b in range(4):
        at = b * TILE_ROWS
        codes = refs[0][at : at + TILE_ROWS, :]
        stacked = jnp.concatenate(
            [codes[:, s * LAT_TILE : (s + 1) * LAT_TILE] for s in range(CAP)], axis=0
        )
        slabs = jnp.dot(pick[...], stacked, preferred_element_type=F32)
        packed = jnp.concatenate(
            [slabs[s * TILE_ROWS : (s + 1) * TILE_ROWS] for s in range(4)], axis=1
        )
        tile_send[:, b] = packed.reshape(32, CAP, 4 * LAT_TILE).astype(BF)


def pack(codes, after):
    whole = pl.BlockSpec(memory_space=pltpu.VMEM)
    return pl.pallas_call(
        pack_kernel,
        in_specs=[whole] * 2 + [ANY] * len(after),
        out_specs=whole,
        out_shape=jax.ShapeDtypeStruct((32, 4, CAP, 4 * LAT_TILE), BF),
        compiler_params=SMALL,
        name="pack",
    )(codes, jnp.asarray(pick_matrix(), BF), *after)


def first_sum_kernel(table, *refs):
    for k in range(3):
        a, b, out = refs[k], refs[3 + k], refs[k - 3]
        out[...] = (a[...].astype(F32) + b[...].astype(F32)).astype(BF)


def first_sum(places, mine, got, after):
    rows = mine.shape[1]
    specs = [
        pl.BlockSpec((1, rows, PIECE), lambda e, p, k=k: (p[PLACES[1] + 4 * k + e], 0, 0))
        for k in range(1, 4)
    ]
    return pl.pallas_call(
        first_sum_kernel,
        grid_spec=pltpu.PrefetchScalarGridSpec(
            num_scalar_prefetch=1,
            grid=(4,),
            in_specs=specs + specs + [ANY] * len(after),
            out_specs=[pl.BlockSpec((1, rows, PIECE), lambda e, p: (e, 0, 0))] * 3,
        ),
        out_shape=[jax.ShapeDtypeStruct((4, rows, PIECE), BF)] * 3,
        compiler_params=SMALL,
        name="first_sum",
    )(places, *([mine] * 3), *([got] * 3), *after)


def second_sum_kernel(table, *refs):
    far = refs[6:9]
    outs = refs[-3:]
    for k in range(3):
        total = refs[k][0].astype(F32) + refs[3 + k][0].astype(F32)
        for ref in far:
            total += ref[k + 1].astype(F32)
        outs[k][...] = total.astype(BF)


def second_sum(places, mine, got, far, after):
    rows = mine.shape[1]
    half = rows
    specs = [
        pl.BlockSpec((1, half, PIECE), lambda i, p, e=e: (p[PLACES[1] + e], i, 0))
        for e in range(1, 4)
    ]
    return pl.pallas_call(
        second_sum_kernel,
        grid_spec=pltpu.PrefetchScalarGridSpec(
            num_scalar_prefetch=1,
            grid=(1,),
            in_specs=specs
            + specs
            + [pl.BlockSpec((4, half, PIECE), lambda i, p: (0, i, 0))] * 3
            + [ANY] * len(after),
            out_specs=[pl.BlockSpec((half, PIECE), lambda i, p: (i, 0))] * 3,
        ),
        out_shape=[jax.ShapeDtypeStruct((rows, PIECE), BF)] * 3,
        compiler_params=LARGE,
        name="second_sum",
    )(places, *([mine] * 3), *([got] * 3), *far, *after)


def error_kernel(table, *refs):
    dec_bias, resid = refs[8:10]
    out, error = refs[-2:]
    total = refs[0][0].astype(F32) + refs[1][0].astype(F32)
    for ref in refs[2:5]:
        total += ref[0].astype(F32)
    for ref in refs[5:8]:
        total += ref[...].astype(F32)
    total += dec_bias[...]
    out[...] = total.astype(BF)
    error[...] = (total - resid[...].astype(F32)).astype(BF)


def error_of(places, mine, got, far, near, dec_bias, resid, after):
    rows = mine.shape[1]
    piece = pl.BlockSpec((rows, PIECE), lambda i, p: (0, 0))
    own = pl.BlockSpec((1, rows, PIECE), lambda i, p: (p[PLACES[1]], 0, 0))
    return pl.pallas_call(
        error_kernel,
        grid_spec=pltpu.PrefetchScalarGridSpec(
            num_scalar_prefetch=1,
            grid=(1,),
            in_specs=[own, own]
            + [pl.BlockSpec((1, rows, PIECE), lambda i, p: (0, 0, 0))] * 3
            + [piece] * 3
            + [pl.BlockSpec((1, PIECE), lambda i, p: (0, p[PLACES[1] + 16])), piece]
            + [ANY] * len(after),
            out_specs=[piece, piece],
        ),
        out_shape=[jax.ShapeDtypeStruct((rows, PIECE), BF)] * 2,
        compiler_params=LARGE,
        name="error",
    )(places, mine, got, *far, *near, dec_bias, resid, *after)


def grad_kernel(ids, places, *refs):
    pieces, codes = refs[: 8 * PARTS], refs[8 * PARTS : 8 * PARTS + 4]
    out, error = refs[-2:]
    n = pl.program_id(0)

    @pl.when(n == 0)
    def _():
        for h in range(PARTS):
            for k in range(8):
                for e in range(4):
                    at = PLACES[0] + 2 * (k * 4 + e)
                    row = pl.multiple_of(places[at] * ROWS + h * HALF, HALF)
                    col = places[at + 1]
                    lane = pl.multiple_of(col % 2 * PIECE, PIECE)
                    error[col // 2, pl.ds(row, HALF), pl.ds(lane, PIECE)] = pieces[8 * h + k][e]

    out[...] = jnp.zeros_like(out)
    for k, shift in enumerate(SHIFTS):
        for b in range(4):
            row = shift * ROWS + b * TILE_ROWS
            part = jnp.dot(
                codes[k][b * 256 : (b + 1) * 256, :],
                error[n, row : row + TILE_ROWS, :],
                preferred_element_type=F32,
            )
            for s in range(CAP):
                at = pl.multiple_of(ids[k * 16 + b * 4 + s] * LAT_TILE, LAT_TILE)
                out[pl.ds(at, LAT_TILE), :] += part[s * LAT_TILE : (s + 1) * LAT_TILE, :]


def grad(ids, places, pieces, codes, after):
    width = 2 * PIECE
    return pl.pallas_call(
        grad_kernel,
        grid_spec=pltpu.PrefetchScalarGridSpec(
            num_scalar_prefetch=2,
            grid=(4,),
            in_specs=[pl.BlockSpec((4, HALF, PIECE), lambda n, *_: (0, 0, 0))] * (8 * PARTS)
            + [pl.BlockSpec((4 * CAP * LAT_TILE + 16, TILE_ROWS), lambda n, *_: (0, 0))] * 4
            + [ANY] * len(after),
            out_specs=pl.BlockSpec((2048, width), lambda n, *_: (0, n)),
            scratch_shapes=[pltpu.VMEM((4, 4 * ROWS, width), BF)],
        ),
        out_shape=jax.ShapeDtypeStruct((2048, 1024), F32),
        compiler_params=LARGE,
        cost_estimate=pl.CostEstimate(
            flops=10**9, bytes_accessed=14 << 20, transcendentals=0
        ),
        name="grad",
    )(ids, places, *pieces, *codes, *after)


def body(residuals, dictionary, enc_bias, dec_bias, tile_ids, tile_counts):
    device = lax.axis_index("tok") * 32 + lax.axis_index("lat")
    places = lax.dynamic_index_in_dim(jnp.asarray(place_table()), device, 0, False)
    ids = tile_ids[:, 0, :]
    counts = tile_counts[:, 0]
    enc_rows = enc_bias.reshape(32, LAT_TILE)
    dec_row = dec_bias.reshape(1, WIDTH)
    halves = range(PARTS)

    line = stack4(short_gather(residuals), [enc_rows, places])
    own = [line] + [send(line, long_leg(d)) for d in SHIFTS[1:]]
    swapped = [send(v, CORE) for v in own[:1]]
    begun = begin(ids, places, own[:2] + swapped, dictionary, dec_row)
    own[3], begun = lax.optimization_barrier((own[3], begun))
    pieces = own + swapped + [send(v, CORE) for v in own[1:]]

    codes, m, other, r = encode(
        ids, counts, places, pieces, begun, dictionary, enc_rows, dec_row
    )
    mine, resid = [m], [r]
    got = [send(other, CORE)]
    sums = [first_sum(places, m, got[0], [])]
    far = [[send(v, long_leg(d)) for v, d in zip(sums[0], SHIFTS[1:])]]

    codes_t = turn(codes, ids, [])
    all_codes = [codes_t] + [
        lax.ppermute(codes_t, "tok", [(z, (z + s) % SIDE) for z in range(SIDE)])
        for s in SHIFTS[1:]
    ]
    all_ids = jnp.concatenate([v[4 * CAP * LAT_TILE, :16] for v in all_codes]).astype(jnp.int32)
    tile_send = pack(codes, [sums[-1][0], codes_t])
    tile_got = lax.all_to_all(tile_send, "lat", split_axis=0, concat_axis=0, tiled=True)
    tile_codes = tile_got.transpose(1, 0, 2, 3)

    recon, error = [], []
    parts = []
    last = tile_send
    for h in halves:
        parts.append(second_sum(places, mine[h], got[h], far[h], [last]))
        last = parts[h][0]
    for h in halves:
        back = [send(v, short_leg(d)) for v, d in zip(parts[h], SHIFTS[1:])]
        r, e = error_of(
            places, mine[h], got[h], far[h], back, dec_row, resid[h],
            [last] if h else [last, all_ids, tile_got],
        )
        last = r
        recon.append(r)
        error.append(e)
    whole = recon[0] if PARTS == 1 else jnp.concatenate(recon)
    error_lines = []
    for h in halves:
        legs = [lax.ppermute(error[h], ("tok", "lat"), plane_leg(d)) for d in SHIFTS]
        error_lines.append(stack4(legs, [last]))
        last = error_lines[h]
    line = error_lines[0]
    own = [line] + [send(line, long_leg(d)) for d in SHIFTS[1:]]
    own[1], whole = lax.optimization_barrier((own[1], whole))
    reconstruction = lax.ppermute(whole, ("tok", "lat"), TO_HOME)
    own[3], reconstruction = lax.optimization_barrier((own[3], reconstruction))
    errors = [own + [send(v, CORE) for v in own]]
    decoder_grad = grad(all_ids, places, sum(errors, []), all_codes, [])
    return (tile_codes, reconstruction, decoder_grad)


def solution(mesh):
    placed = (
        P("tok", "lat"),
        P("lat", None),
        P("lat"),
        P(),
        P("tok", "lat", None),
        P("tok", "lat"),
    )
    return jax.shard_map(
        body,
        mesh=mesh,
        in_specs=placed,
        out_specs=(P("tok", None, None, "lat"), P("tok", "lat"), P("lat", "tok")),
        check_vma=False,
    )
```
